32 devices in a mesh: branch: 2 (over core), prow: 8 (over z, x), pcol: 2 (over y).
Axes of the slice: x: 2, y: 2, z: 4, core: 2. Of those that a mesh axis runs over, the one named last changes fastest.
Arguments:
- pair_rep: float32 [128, 128, 128], P(('branch', 'prow'), 'pcol'), may hold values from -6 to 6
- alignment: float32 [8, 128, 256], P('pcol', ('branch', 'prow')), may hold values from -6 to 6
- residue_mask: int32 [128], replicated, may hold values 0 or 1
- row_mask: int32 [8, 128], P('pcol', ('branch', 'prow')), may hold values 0 or 1
- attention_in: float32 [256, 1024], replicated, may hold values from -0.375 to 0.375
- pair_bias_w: float32 [128, 8], replicated, may hold values from -40 to 40
- attention_out: float32 [256, 256], replicated, may hold values from -0.375 to 0.375
- outer_in: float32 [256, 64], replicated, may hold values from -0.375 to 0.375
- outer_out: float32 [1024, 128], replicated, may hold values from -0.1875 to 0.1875
- triangle_in: float32 [128, 512], replicated, may hold values from -0.5 to 0.5
- triangle_gate: float32 [128, 128], replicated, may hold values from -0.5 to 0.5
- triangle_out: float32 [128, 128], replicated, may hold values from -0.5 to 0.5
- transit_in: float32 [128, 512], replicated, may hold values from -0.5 to 0.5
- transit_out: float32 [512, 128], replicated, may hold values from -0.25 to 0.25
Outputs:
- new_alignment: float32 [8, 128, 256], P('pcol', ('branch', 'prow'))
- new_pair: float32 [128, 128, 128], P(('branch', 'prow'), 'pcol')
The draws below stay inside these ranges and needn't reach their ends.
All inputs are finite; a program needn't handle non-finite values. No bound on the sum of `row_mask` on one device may be relied on, other than what follows from the above.
Results may differ from the reference program's by a relative error of at most 0.0003.
Values sent between devices are 32-bit elements; how exact they have to be, the bound alone decides.
A program may use at most 64 MiB of HBM per device.

```python
import jax
import jax.numpy as jnp
from jax import lax

CZ = 128
CM = 256
HEADS = 8
TRI = 128
TRANS = 512
OUTER = 32
ATT = 256
R = 128
S = 8


def draw_pair_bias_w(key, part):
    sample = jax.random.normal(key, (CZ, HEADS), jnp.float32)
    sample = sample * (2.0 / CZ ** 0.5)
    return jnp.clip(sample, -40.0, 40.0)


def place_ends(entries, stream_key, low, top_value):
    spot = [jax.random.randint(jax.random.fold_in(stream_key, axis), (), 0, length) for axis, length in enumerate(entries.shape)]
    longest = entries.shape.index(max(entries.shape))
    beside = spot[:longest] + [(spot[longest] + 1) % entries.shape[longest]] + spot[longest + 1:]
    return entries.at[tuple(spot)].set(low).at[tuple(beside)].set(top_value)


def block_scale(key, dims, split, low, largest):
    level, own = 1.0, jax.random.fold_in(key, 6)
    for dim, shards_of in split:
        heights = jnp.exp(jax.random.uniform(jax.random.fold_in(own, dim), (shards_of,), jnp.float32, low / len(split), largest / len(split)))
        level = level * jnp.repeat(heights, dims[dim] // shards_of).reshape([-1 if axis == dim else 1 for axis in range(len(dims))])
    return level


def noise(key, extent, deviation, reach, shards=(), held_as=jnp.bfloat16):
    factor_of = block_scale(key, extent, shards, -0.22, 0.18) if shards else 1.0
    result = jax.random.normal(key, extent, jnp.float32) * deviation * factor_of
    return jnp.minimum(jnp.maximum(result, -reach), reach).astype(held_as)


def setup_inputs(seed: int = 0) -> dict:
    keys = jax.random.split(jax.random.key(seed), 15)
    pair_rep = noise(keys[0], (R, R, CZ), 1.0, 6.0, ((0, 16), (1, 2)), jnp.float32)
    alignment = noise(keys[1], (S, R, CM), 1.0, 6.0, ((0, 2), (1, 16)), jnp.float32)
    residue_mask = place_ends((jax.random.randint(keys[2], (R,), 0, 8) < 7).astype(jnp.int32), jax.random.fold_in(keys[2], 1), 0, 1)
    row_mask = place_ends((jax.random.randint(keys[3], (S, R), 0, 4) < 3).astype(jnp.int32), jax.random.fold_in(keys[3], 1), 0, 1)
    attention_in = noise(keys[4], (CM, 4 * ATT), CM ** -0.5, 0.375, (), jnp.float32)
    pair_bias_w = draw_pair_bias_w(jax.random.fold_in(keys[14], 71), 0)
    attention_out = noise(keys[6], (ATT, CM), ATT ** -0.5, 0.375, (), jnp.float32)
    outer_in = noise(keys[7], (CM, 2 * OUTER), CM ** -0.5, 0.375, (), jnp.float32)
    outer_out = noise(keys[8], (OUTER * OUTER, CZ), (OUTER * OUTER) ** -0.5, 0.1875, (), jnp.float32)
    triangle_in = noise(keys[9], (CZ, 4 * TRI), CZ ** -0.5, 0.5, (), jnp.float32)
    triangle_gate = noise(keys[10], (CZ, CZ), CZ ** -0.5, 0.5, (), jnp.float32)
    triangle_out = noise(keys[11], (TRI, CZ), TRI ** -0.5, 0.5, (), jnp.float32)
    transit_in = noise(keys[12], (CZ, TRANS), CZ ** -0.5, 0.5, (), jnp.float32)
    transit_out = noise(keys[13], (TRANS, CZ), TRANS ** -0.5, 0.25, (), jnp.float32)
    return dict(pair_rep=pair_rep, alignment=alignment, residue_mask=residue_mask, row_mask=row_mask, attention_in=attention_in, pair_bias_w=pair_bias_w, attention_out=attention_out, outer_in=outer_in, outer_out=outer_out, triangle_in=triangle_in, triangle_gate=triangle_gate, triangle_out=triangle_out, transit_in=transit_in, transit_out=transit_out)


highest = lax.Precision.HIGHEST
epsilon = 1e-05

def layer_norm(values):
    center = values - lax.optimization_barrier(jnp.mean(values, axis=-1, keepdims=True))
    spread = lax.optimization_barrier(jnp.mean(center * center, axis=-1, keepdims=True))
    return center * lax.rsqrt(spread + epsilon)

def matmul(left_side, right_side):
    return jnp.dot(left_side, right_side, precision=highest, preferred_element_type=jnp.float32)

def reference(pair_rep, alignment, residue_mask, row_mask, attention_in, pair_bias_w, attention_out, outer_in, outer_out, triangle_in, triangle_gate, triangle_out, transit_in, transit_out):
    res_count = alignment.shape[1]
    head_count = pair_bias_w.shape[1]
    att_width = attention_out.shape[0]
    head_depth = att_width // head_count
    outer_width = outer_in.shape[1] // 2
    inner_width = triangle_out.shape[0]
    normed = layer_norm(alignment)
    projected = matmul(normed, attention_in)
    queries = projected[..., :att_width] * head_depth ** (-0.5)
    key_vals = projected[..., att_width:2 * att_width]
    value_vals = projected[..., 2 * att_width:3 * att_width]
    gate_logits = projected[..., 3 * att_width:]
    pair_norm = layer_norm(pair_rep)
    pair_bias = jnp.einsum('ijc,ch->hij', pair_norm, pair_bias_w, precision=highest)
    mask_float = row_mask.astype(jnp.float32)
    key_bias = 1000000000.0 * (mask_float - 1.0)

    def attend_row(items):
        query_row, key_row, value_row, bias_row = items
        query_row = query_row.reshape(res_count, head_count, head_depth)
        key_row = key_row.reshape(res_count, head_count, head_depth)
        value_row = value_row.reshape(res_count, head_count, head_depth)
        scores = jnp.einsum('ihd,jhd->hij', query_row, key_row, precision=highest) + pair_bias + bias_row[None, None, :]
        scores = scores - lax.optimization_barrier(jnp.max(scores, axis=-1, keepdims=True))
        weights = jnp.exp(scores)
        weights = weights / lax.optimization_barrier(jnp.sum(weights, axis=-1, keepdims=True))
        mixed = jnp.einsum('hij,jhd->ihd', weights, value_row, precision=highest)
        return mixed.reshape(res_count, att_width)
    attended = lax.map(attend_row, (queries, key_vals, value_vals, key_bias))
    new_alignment = alignment + matmul(attended * jax.nn.sigmoid(gate_logits), attention_out)
    factors = matmul(layer_norm(new_alignment), outer_in) * mask_float[..., None]
    left_outer = factors[..., :outer_width]
    right_outer = factors[..., outer_width:]
    counts = 1.0 + matmul(mask_float.T, mask_float)

    def outer_row(left_row):
        product = jnp.einsum('sp,sjq->jpq', left_row, right_outer, precision=highest)
        return matmul(product.reshape(res_count, outer_width * outer_width), outer_out)
    outer_sum = lax.map(outer_row, jnp.transpose(left_outer, (1, 0, 2)))
    outer_mean = outer_sum / counts[..., None]
    pair_one = pair_rep + outer_mean
    tri_norm = layer_norm(pair_one)
    res_float = residue_mask.astype(jnp.float32)
    pair_valid = (res_float[:, None] * res_float[None, :])[..., None]
    edges = matmul(tri_norm, triangle_in)
    left_edge = jax.nn.sigmoid(edges[..., :inner_width]) * edges[..., inner_width:2 * inner_width] * pair_valid
    right_edge = jax.nn.sigmoid(edges[..., 2 * inner_width:3 * inner_width]) * edges[..., 3 * inner_width:] * pair_valid
    crossed = jnp.einsum('ikc,jkc->ijc', left_edge, right_edge, precision=highest)
    triangle = matmul(layer_norm(crossed), triangle_out) * jax.nn.sigmoid(matmul(tri_norm, triangle_gate))
    pair_mid = pair_one + triangle
    hidden_units = jax.nn.relu(matmul(layer_norm(pair_mid), transit_in))
    new_pair = pair_mid + matmul(hidden_units, transit_out)
    return (new_alignment, new_pair)
```

```python
import functools

import jax
import jax.numpy as jnp
import numpy as np
from jax import lax
from jax.experimental import pallas as pl
from jax.experimental.pallas import tpu as pltpu
from jax.sharding import PartitionSpec as P

MESH = pl.DeviceIdType.MESH
NN = (((1,), (0,)), ((), ()))
NT = (((1,), (1,)), ((), ()))

highest = lax.Precision.HIGHEST
epsilon = 1e-05


def layer_norm(values):
    center = values - jnp.mean(values, axis=-1, keepdims=True)
    spread = jnp.mean(center * center, axis=-1, keepdims=True)
    return center * lax.rsqrt(spread + epsilon)


def matmul(left_side, right_side):
    return jnp.dot(left_side, right_side, precision=highest, preferred_element_type=jnp.float32)


def outer_block(left_rows, right_cols, outer_out):
    product = jnp.einsum("sip,sjq->ijpq", left_rows, right_cols, precision=highest)
    row_total, col_total, left_width, right_width = product.shape
    return matmul(product.reshape(row_total, col_total, left_width * right_width), outer_out)


def shards(
    pair_rep,
    alignment,
    residue_mask,
    row_mask,
    attention_in,
    pair_bias_w,
    attention_out,
    outer_in,
    outer_out,
    triangle_in,
    triangle_gate,
    triangle_out,
    transit_in,
    transit_out,
):
    row_count, col_count, _ = pair_rep.shape
    seq_count = alignment.shape[0]
    head_count = pair_bias_w.shape[1]
    att_width = attention_out.shape[0]
    head_depth = att_width // head_count
    outer_width = outer_in.shape[1] // 2
    inner_width = triangle_out.shape[0]
    row_start = lax.axis_index(("branch", "prow")) * row_count
    col_start = lax.axis_index("pcol") * col_count
    pair_norm = layer_norm(pair_rep)
    bias_tile = jnp.einsum("ijc,ch->hij", pair_norm, pair_bias_w, precision=highest)
    bias_rows = lax.all_gather(bias_tile, "pcol", axis=2, tiled=True)
    normed = layer_norm(alignment)
    mask_float = row_mask.astype(jnp.float32)
    key_bias = 1000000000.0 * (mask_float - 1.0)
    queries = matmul(normed, attention_in[:, :att_width]) * head_depth ** (-0.5)
    queries = queries.reshape(seq_count, row_count, head_count, head_depth)
    gate_logits = matmul(normed, attention_in[:, 3 * att_width :])
    key_value_w = attention_in[:, att_width : 3 * att_width]
    key_value_local = matmul(normed, key_value_w)
    widen = lambda sent_block: sent_block
    running_max = jnp.full((seq_count, head_count, row_count), -1e30, jnp.float32)
    make_sent_block = lax.all_gather(key_value_local, ("branch", "prow"), axis=1, tiled=True)
    block_bias = lax.all_gather(key_bias, ("branch", "prow"), axis=1, tiled=True)
    key_value = widen(make_sent_block)
    key_count = block_bias.shape[1]
    key_block = key_value[..., :att_width].reshape(seq_count, key_count, head_count, head_depth)
    value_block = key_value[..., att_width:].reshape(seq_count, key_count, head_count, head_depth)
    scores = jnp.einsum("sihd,sjhd->shij", queries, key_block, precision=highest)
    scores = scores + bias_rows[None] + block_bias[:, None, None, :]
    block_max = jnp.maximum(running_max, jnp.max(scores, axis=-1))
    weights = jnp.exp(scores - block_max[..., None])
    running_sum = jnp.sum(weights, axis=-1)
    accumulated = jnp.einsum("shij,sjhd->shid", weights, value_block, precision=highest)
    final_state = (block_max, running_sum, accumulated)
    _, running_sum, accumulated = final_state
    mixed = accumulated / running_sum[..., None]
    mixed = jnp.transpose(mixed, (0, 2, 1, 3)).reshape(seq_count, row_count, att_width)
    new_alignment = alignment + matmul(mixed * jax.nn.sigmoid(gate_logits), attention_out)
    factors = matmul(layer_norm(new_alignment), outer_in) * mask_float[..., None]
    left_outer = factors[..., :outer_width]
    right_outer = factors[..., outer_width:]
    right_all, mask_all = (
        lax.all_gather(right_outer, ("branch", "prow"), axis=1, tiled=True),
        lax.all_gather(mask_float, ("branch", "prow"), axis=1, tiled=True),
    )
    left_full, left_mask = (
        lax.all_gather(left_outer, "pcol", axis=0, tiled=True),
        lax.all_gather(mask_float, "pcol", axis=0, tiled=True),
    )
    right_tile, mask_tile = (
        lax.all_to_all(right_all, "pcol", split_axis=1, concat_axis=0, tiled=True),
        lax.all_to_all(mask_all, "pcol", split_axis=1, concat_axis=0, tiled=True),
    )
    outer_sum = outer_block(left_full, right_tile, outer_out)
    count_sum = jnp.einsum("si,sj->ij", left_mask, mask_tile, precision=highest)
    outer_mean = outer_sum / (1.0 + count_sum)[..., None]
    pair_one = pair_rep + outer_mean
    tri_norm = layer_norm(pair_one)
    res_float = residue_mask.astype(jnp.float32)
    row_valid = lax.dynamic_slice_in_dim(res_float, row_start, row_count)
    col_valid = lax.dynamic_slice_in_dim(res_float, col_start, col_count)
    pair_valid = (row_valid[:, None] * col_valid[None, :])[..., None]
    edges = matmul(tri_norm, triangle_in)
    left_edge = (
        jax.nn.sigmoid(edges[..., :inner_width])
        * edges[..., inner_width : 2 * inner_width]
        * pair_valid
    )
    right_edge = (
        jax.nn.sigmoid(edges[..., 2 * inner_width : 3 * inner_width])
        * edges[..., 3 * inner_width :]
        * pair_valid
    )
    cross_part = jnp.einsum(
        "ikc,jkc->ijc",
        left_edge,
        lax.all_gather(right_edge, ("branch", "prow"), axis=0, tiled=True),
        precision=highest,
    )
    crossed = lax.psum_scatter(cross_part, "pcol", scatter_dimension=1, tiled=True)
    triangle = matmul(layer_norm(crossed), triangle_out) * jax.nn.sigmoid(
        matmul(tri_norm, triangle_gate)
    )
    pair_mid = pair_one + triangle
    hidden_units = jax.nn.relu(matmul(layer_norm(pair_mid), transit_in))
    new_pair = pair_mid + matmul(hidden_units, transit_out)
    return (new_alignment, new_pair)


def split(values):
    high = values.astype(jnp.bfloat16)
    return high, (values - high.astype(jnp.float32)).astype(jnp.bfloat16)


def dot(a, b, dims=NN):
    return lax.dot_general(a, b, dims, preferred_element_type=jnp.float32)


def dot_split(a, b, dims=NN):
    return dot(a[0], b[0], dims) + (dot(a[0], b[1], dims) + dot(a[1], b[0], dims))


def mm(a, b, dims=NN):
    return dot_split(split(a), split(b), dims)


def mm_high(a, b, dims=NN):
    return lax.dot_general(a, b, dims, precision=highest, preferred_element_type=jnp.float32)


def sigmoid(v):
    return 1.0 / (1.0 + jnp.exp(-v))


def pick(matrix, pair, dims=NN):
    return tuple(dot(matrix, part, dims).astype(jnp.bfloat16) for part in pair)


def pick_right(pair, matrix):
    return tuple(dot(part, matrix).astype(jnp.bfloat16) for part in pair)


def block_kernel(
    sizes,
    pair_ref, ali_ref, res_ref, row_ref, ain_ref, pbw_ref, aout_ref, oin_ref, oout_ref,
    tin_ref, tgate_ref, tout_ref, xin_ref, xout_ref,
    perm_outer_ref, perm_gate_ref, perm_value_ref, perm_row_ref, pos_ref,
    nali_ref, npair_ref,
    qsend, qrecv, bsend, brecv, msend, mrecv, frs, frr, fls, flr, es, er, cs, cr,
    lsc, tsc, p1, xs, send_sem, recv_sem,
):
    nb, np_, nc = sizes
    nr = nb * np_
    nd = nr * nc
    rb, cb, cz = pair_ref.shape
    sb, _, cm = ali_ref.shape
    seq = sb * nc
    res = rb * nr
    heads = pbw_ref.shape[1]
    att = aout_ref.shape[0]
    depth = att // heads
    groups = nr // sb
    hpg = heads // groups
    gw = hpg * depth
    ow = oin_ref.shape[1] // 2
    tri = tout_ref.shape[0]
    cpd = tri // nd
    per = nr // nc
    pos = rb * cb
    nib = pos // 128
    f32 = jnp.float32

    r_me = lax.axis_index("branch") * np_ + lax.axis_index("prow")
    p_me = lax.axis_index("pcol")
    me = r_me * nc + p_me

    def where(r, p):
        return {"branch": r // np_, "prow": lax.rem(r, np_), "pcol": p}

    def al(v, m):
        return pl.multiple_of(v, m)

    def copy(phase, src, dst, tag, origin, r, p):
        return pltpu.make_async_remote_copy(
            src_ref=src, dst_ref=dst, send_sem=send_sem.at[phase, tag],
            recv_sem=recv_sem.at[phase, origin], device_id=where(r, p), device_id_type=MESH,
        )

    barrier = pltpu.get_barrier_semaphore()

    @pl.loop(1, nd)
    def _(k):
        t = lax.rem(me + k, nd)
        pl.semaphore_signal(barrier, inc=1, device_id=where(t // nc, lax.rem(t, nc)), device_id_type=MESH)

    pair = pair_ref[...].reshape(pos, cz)
    pair_norm = layer_norm(pair)
    for i in range(rb):
        bsend[:, i, :] = mm_high(pbw_ref[...].T, pair_norm[i * cb : (i + 1) * cb], NT)

    pl.semaphore_wait(barrier, nd - 1)

    def b_copy(r, p, origin_r, origin_p):
        group = lax.rem(r, groups)
        return copy(
            1, bsend.at[pl.ds(group * hpg, hpg)],
            brecv.at[origin_p, :, pl.ds(al(origin_r * rb, rb), rb), :],
            r * nc + p, origin_r * nc + origin_p, r, p,
        )

    @pl.loop(1, nd)
    def _(k):
        t = lax.rem(me + k, nd)
        b_copy(t // nc, lax.rem(t, nc), r_me, p_me).start()

    brecv[p_me, :, pl.ds(al(r_me * rb, rb), rb), :] = bsend[pl.ds(lax.rem(r_me, groups) * hpg, hpg)]

    ali = ali_ref[...].reshape(sb * rb, cm)
    projected = mm_high(layer_norm(ali), ain_ref[...])
    gate = sigmoid(projected[:, 3 * att :])
    mask = row_ref[...].astype(f32)
    eye = (
        lax.broadcasted_iota(jnp.int32, (rb, rb), 0) == lax.broadcasted_iota(jnp.int32, (rb, rb), 1)
    ).astype(f32)
    mask_cols = [jnp.sum(eye * mask[s : s + 1, :], axis=1, keepdims=True) for s in range(sb)]
    for s in range(sb):
        rows = projected[s * rb : (s + 1) * rb]
        for g in range(groups):
            for n in range(3):
                qsend[s * groups + g, :, n * gw : (n + 1) * gw] = rows[
                    :, n * att + g * gw : n * att + (g + 1) * gw
                ]
            qsend[s * groups + g, :, 3 * gw :] = jnp.broadcast_to(mask_cols[s], (rb, gw))

    def q_copy(r, origin_r):
        return copy(
            0, qsend.at[r], qrecv.at[pl.ds(al(origin_r * rb, rb), rb), :], r, origin_r, r, p_me
        )

    @pl.loop(1, nr)
    def _(k):
        q_copy(lax.rem(r_me + k, nr), r_me).start()

    qrecv[pl.ds(al(r_me * rb, rb), rb), :] = qsend[r_me]

    tin = split(tin_ref[...])
    w_gate = pick(perm_gate_ref[...], tin, NT)
    w_value = pick(perm_value_ref[...], tin, NT)
    res_rows = jnp.broadcast_to(res_ref[...].astype(f32), (8, res)).astype(jnp.bfloat16)
    index = lax.broadcasted_iota(jnp.int32, (res, pos), 0)
    row_pick = (index == pos_ref[0:1, :] + r_me * rb).astype(jnp.bfloat16)
    col_pick = (index == pos_ref[1:2, :] + p_me * cb).astype(jnp.bfloat16)
    valid = (dot(res_rows, row_pick) * dot(res_rows, col_pick))[0:1, :]

    @pl.loop(1, nr)
    def _(k):
        q_copy(r_me, lax.rem(r_me + k, nr)).wait_recv()

    @pl.loop(1, nd)
    def _(k):
        t = lax.rem(me + k, nd)
        b_copy(r_me, p_me, t // nc, lax.rem(t, nc)).wait_recv()

    first = (lax.broadcasted_iota(jnp.int32, (8, gw), 1) == 0).astype(f32)
    mask_row = dot(first.astype(jnp.bfloat16), qrecv[:, 3 * gw :].astype(jnp.bfloat16), NT)[0:1]
    key_bias = 1000000000.0 * (mask_row - 1.0)
    for h in range(hpg):
        queries = qrecv[:, h * depth : (h + 1) * depth] * depth ** (-0.5)
        keys = qrecv[:, gw + h * depth : gw + (h + 1) * depth]
        vals = qrecv[:, 2 * gw + h * depth : 2 * gw + (h + 1) * depth]
        bias = jnp.concatenate([brecv[p, h] for p in range(nc)], axis=1)
        scores = mm_high(queries, keys, NT) + bias + key_bias
        weights = jnp.exp(scores - jnp.max(scores, axis=1, keepdims=True))
        total = jnp.sum(weights, axis=1, keepdims=True)
        msend[:, h * depth : (h + 1) * depth] = mm(weights, vals) / total

    def m_copy(r, origin_r):
        return copy(
            2, msend.at[pl.ds(al(r * rb, rb), rb), :], mrecv.at[origin_r], r, origin_r, r, p_me
        )

    @pl.loop(1, nr)
    def _(k):
        m_copy(lax.rem(r_me + k, nr), r_me).start()

    mrecv[r_me] = msend[pl.ds(al(r_me * rb, rb), rb), :]

    @pl.loop(1, nr)
    def _(k):
        m_copy(r_me, lax.rem(r_me + k, nr)).wait_recv()

    mixed = jnp.concatenate(
        [
            jnp.concatenate([mrecv[s * groups + g] for g in range(groups)], axis=1)
            for s in range(sb)
        ],
        axis=0,
    )
    new_ali = ali + mm(mixed * gate, aout_ref[...])
    factors = mm(layer_norm(new_ali), oin_ref[...])
    width = sb * ow
    lane = lax.broadcasted_iota(jnp.int32, (rb, 128), 1)
    mask_lanes = jnp.zeros((rb, 128), f32)
    for s in range(sb):
        part = factors[s * rb : (s + 1) * rb] * mask_cols[s]
        fls[:, s * ow : (s + 1) * ow] = part[:, :ow]
        frs[:, s * ow : (s + 1) * ow] = part[:, ow:]
        mask_lanes = jnp.where(lane == s, mask_cols[s], mask_lanes)
    fls[:, width:] = mask_lanes
    frs[:, width:] = mask_lanes
    home = r_me // per

    def fr_copy(r, p, origin_r, origin_p):
        return copy(
            3, frs, frr.at[origin_p, pl.ds(al(lax.rem(origin_r, per) * rb, rb), rb), :],
            r, origin_r * nc + origin_p, r, p,
        )

    def fl_copy(p, origin_p):
        return copy(4, fls, flr.at[origin_p], p, origin_p, r_me, p)

    @pl.loop(0, nr)
    def _(k):
        r = lax.rem(r_me + k, nr)

        @pl.when(jnp.logical_or(r != r_me, home != p_me))
        def _():
            fr_copy(r, home, r_me, p_me).start()

    for k in range(1, nc):
        fl_copy(lax.rem(p_me + k, nc), p_me).start()

    nali_ref[...] = new_ali.reshape(sb, rb, cm)

    @pl.when(home == p_me)
    def _():
        frr[p_me, pl.ds(al(lax.rem(r_me, per) * rb, rb), rb), :] = frs[...]

    flr[p_me] = fls[...]

    for k in range(1, nc):
        fl_copy(p_me, lax.rem(p_me + k, nc)).wait_recv()

    for p in range(nc):
        for s in range(sb):
            lsc[pl.ds(p * sb + s, rb, stride=seq), :] = jnp.concatenate(
                [flr[p, :, s * ow : (s + 1) * ow], jnp.zeros((rb, 128 - ow), f32)], axis=1
            )
    left = lsc[:, :ow]
    left_high, left_low = split(left)
    left_cat = jnp.concatenate([left_high, left_low, left_high], axis=1)
    for q in range(ow):
        w_high, w_low = split(oout_ref[pl.ds(q, ow, stride=ow), :])
        w_cat = jnp.concatenate([w_high, w_high, w_low], axis=0)
        tsc[:, q, :, :] = dot(left_cat, w_cat).reshape(rb, seq, cz)

    @pl.loop(0, per * nc)
    def _(k):
        origin_r = p_me * per + k // nc
        origin_p = lax.rem(k, nc)

        @pl.when(jnp.logical_or(origin_r != r_me, origin_p != p_me))
        def _():
            fr_copy(r_me, p_me, origin_r, origin_p).wait_recv()

    right = pick_right(
        split(jnp.concatenate([frr[p, :, :width] for p in range(nc)], axis=1)), perm_outer_ref[...]
    )
    mask_right = jnp.concatenate([frr[p, :, width : width + sb] for p in range(nc)], axis=1)
    mask_left = jnp.concatenate([flr[p, :, width : width + sb] for p in range(nc)], axis=1)
    for i in range(rb):
        outer = dot_split(right, split(tsc[i].reshape(ow * seq, cz)))
        count = jnp.sum(mask_right * mask_left[i : i + 1, :], axis=1, keepdims=True)
        p1[i * cb : (i + 1) * cb, :] = pair_ref[i] + outer / (1.0 + count)
    pair_one = p1[...]
    tri_norm = layer_norm(pair_one)
    tri_split = split(tri_norm)
    edge = sigmoid(dot_split(w_gate, tri_split, NT)) * dot_split(w_value, tri_split, NT) * valid
    for b in range(nib):
        es[b] = edge[:, b * 128 : (b + 1) * 128]

    rows_each = 2 * cpd

    def e_copy(r, p, origin_r, origin_p):
        return copy(
            5, es.at[:, pl.ds(al((r * nc + p) * rows_each, rows_each), rows_each), :],
            er.at[:, pl.ds(al((origin_p * nr + origin_r) * rows_each, rows_each), rows_each), :],
            r * nc + p, origin_r * nc + origin_p, r, p,
        )

    @pl.loop(1, nd)
    def _(k):
        t = lax.rem(me + k, nd)
        e_copy(t // nc, lax.rem(t, nc), r_me, p_me).start()

    er[:, pl.ds(al((p_me * nr + r_me) * rows_each, rows_each), rows_each), :] = es[
        :, pl.ds(al(me * rows_each, rows_each), rows_each), :
    ]
    out_gate = sigmoid(dot_split(tri_split, split(tgate_ref[...])))

    @pl.loop(1, nd)
    def _(k):
        t = lax.rem(me + k, nd)
        e_copy(r_me, p_me, t // nc, lax.rem(t, nc)).wait_recv()

    def edge_matrix(row):
        blocks = []
        per_lane = 128 // cb
        for b in range(nib):
            halves = [er[b, pl.ds(p * nr * rows_each + row, nr, stride=rows_each), :] for p in range(nc)]
            for n in range(per_lane):
                blocks.append(
                    jnp.concatenate([half[:, n * cb : (n + 1) * cb] for half in halves], axis=1)
                )
        return pick(perm_row_ref[...], split(jnp.concatenate(blocks, axis=0)))

    for c in range(cpd):
        crossed = dot_split(edge_matrix(c), edge_matrix(cpd + c), NT)
        for p in range(nc):
            cs[p, c] = crossed[:, p * cb : (p + 1) * cb]

    def c_copy(r, p, origin):
        return copy(
            6, cs.at[p, :, pl.ds(al(r * rb, rb), rb), :], cr.at[pl.ds(origin * cpd, cpd)],
            r * nc + p, origin, r, p,
        )

    @pl.loop(1, nd)
    def _(k):
        t = lax.rem(me + k, nd)
        c_copy(t // nc, lax.rem(t, nc), me).start()

    cr[pl.ds(me * cpd, cpd)] = cs[p_me, :, pl.ds(al(r_me * rb, rb), rb), :]

    @pl.loop(1, nd)
    def _(k):
        t = lax.rem(me + k, nd)
        c_copy(r_me, p_me, t).wait_recv()

    crossed = cr[...]
    center = crossed - jnp.mean(crossed, axis=0, keepdims=True)
    spread = jnp.mean(center * center, axis=0, keepdims=True)
    normed = (center * lax.rsqrt(spread + epsilon)).reshape(tri * rb, cb)
    xs[...] = jnp.concatenate([normed] * (128 // cb), axis=1)
    w_out = split(tout_ref[...])
    tri_rows = []
    for i in range(rb):
        flipped = xs[pl.ds(i, tri, stride=rb), :].T[:cb]
        tri_rows.append(dot_split(split(flipped), w_out))
    triangle = jnp.concatenate(tri_rows, axis=0) * out_gate
    pair_mid = pair_one + triangle
    hidden = jnp.maximum(mm(layer_norm(pair_mid), xin_ref[...]), 0.0)
    npair_ref[...] = (pair_mid + mm(hidden, xout_ref[...])).reshape(rb, cb, cz)

    @pl.loop(1, nr)
    def _(k):
        r = lax.rem(r_me + k, nr)
        q_copy(r, r_me).wait_send()
        m_copy(r, r_me).wait_send()

    @pl.loop(0, nr)
    def _(k):
        r = lax.rem(r_me + k, nr)

        @pl.when(jnp.logical_or(r != r_me, home != p_me))
        def _():
            fr_copy(r, home, r_me, p_me).wait_send()

    for k in range(1, nc):
        fl_copy(lax.rem(p_me + k, nc), p_me).wait_send()

    @pl.loop(1, nd)
    def _(k):
        t = lax.rem(me + k, nd)
        b_copy(t // nc, lax.rem(t, nc), r_me, p_me).wait_send()
        e_copy(t // nc, lax.rem(t, nc), r_me, p_me).wait_send()
        c_copy(t // nc, lax.rem(t, nc), me).wait_send()


def fused(sizes, *args):
    (pair, ali, res_mask, row_mask, ain, pbw, aout, oin, oout, tin, tgate, tout, xin, xout) = args
    nb, np_, nc = sizes
    nr = nb * np_
    nd = nr * nc
    rb, cb, cz = pair.shape
    sb, _, cm = ali.shape
    res = rb * nr
    seq = sb * nc
    heads = pbw.shape[1]
    depth = aout.shape[0] // heads
    groups = nr // sb
    hpg = heads // groups
    gw = hpg * depth
    ow = oin.shape[1] // 2
    tri = tout.shape[0]
    cpd = tri // nd
    pos = rb * cb
    f32 = jnp.float32

    a = np.arange(seq * ow)
    perm_outer = np.zeros((seq * ow, seq * ow), np.float32)
    perm_outer[a, (a % ow) * seq + a // ow] = 1.0
    row = np.arange(2 * tri)
    channel = (row // cpd % 2) * 2 * tri + (row // (2 * cpd)) * cpd + row % cpd
    perm_gate = np.zeros((2 * tri, 4 * tri), np.float32)
    perm_gate[row, channel] = 1.0
    perm_value = np.zeros((2 * tri, 4 * tri), np.float32)
    perm_value[row, channel + tri] = 1.0
    n = np.arange(res)
    perm_row = np.zeros((res, res), np.float32)
    perm_row[n, (n % rb) * nr + n // rb] = 1.0
    position = np.arange(pos)
    pos_table = np.stack([position // cb, position % cb]).astype(np.int32)
    consts = [jnp.asarray(m, jnp.bfloat16) for m in (perm_outer, perm_gate, perm_value, perm_row)]
    operands = [
        pair, ali, res_mask.reshape(1, res), row_mask, ain, pbw, aout, oin, oout, tin, tgate, tout,
        xin, xout, *consts, jnp.asarray(pos_table),
    ]
    vmem = pl.BlockSpec(memory_space=pltpu.VMEM)
    fw = sb * ow + 128
    scratch = [
        ((nr, rb, 4 * gw)), ((res, 4 * gw)),
        ((heads, rb, cb)), ((nc, hpg, res, cb)),
        ((res, gw)), ((nr, rb, gw)),
        ((rb, fw)), ((nc, cb, fw)), ((rb, fw)), ((nc, rb, fw)),
        ((pos // 128, 2 * tri, 128)), ((pos // 128, 2 * tri, 128)),
        ((nc, cpd, res, cb)), ((tri, rb, cb)),
        ((rb * seq, 128)), ((rb, ow, seq, cz)), ((pos, cz)), ((tri * rb, 128)),
    ]
    return pl.pallas_call(
        functools.partial(block_kernel, sizes),
        out_shape=(
            jax.ShapeDtypeStruct(ali.shape, f32),
            jax.ShapeDtypeStruct(pair.shape, f32),
        ),
        in_specs=[vmem] * len(operands),
        out_specs=(vmem, vmem),
        scratch_shapes=[pltpu.VMEM(s, f32) for s in scratch]
        + [pltpu.SemaphoreType.DMA((7, nd)), pltpu.SemaphoreType.DMA((7, nd))],
        compiler_params=pltpu.CompilerParams(
            collective_id=0, has_side_effects=True, vmem_limit_bytes=48 * 1024 * 1024
        ),
    )(*operands)


def fits(sizes, args):
    pair, ali, pbw, aout, oin, tout = (args[n] for n in (0, 1, 5, 6, 7, 11))
    nb, np_, nc = sizes
    nr = nb * np_
    rb, cb, cz = pair.shape
    sb = ali.shape[0]
    heads = pbw.shape[1]
    depth = aout.shape[0] // heads
    if nr % sb or heads % (nr // sb) or nr % nc or tout.shape[0] % (nr * nc):
        return False
    return (
        ali.shape[1] == rb and rb % 8 == 0 and cb * nc == rb * nr and 128 % cb == 0 and cz == 128
        and (sb * nc) % 8 == 0 and (2 * (tout.shape[0] // (nr * nc))) % 8 == 0
        and (heads // (nr // sb)) * depth * 4 % 128 == 0 and sb * (oin.shape[1] // 2) % 128 == 0
        and (rb * cb) % 128 == 0
    )


def solution(mesh):
    sizes = tuple(mesh.shape[name] for name in ("branch", "prow", "pcol"))

    def local(*args):
        if fits(sizes, args):
            return fused(sizes, *args)
        return shards(*args)

    return jax.shard_map(
        local,
        mesh=mesh,
        in_specs=(
            P(("branch", "prow"), "pcol", None),
            P("pcol", ("branch", "prow"), None),
            P(),
            P("pcol", ("branch", "prow")),
            P(),
            P(),
            P(),
            P(),
            P(),
            P(),
            P(),
            P(),
            P(),
            P(),
        ),
        out_specs=(P("pcol", ("branch", "prow"), None), P(("branch", "prow"), "pcol", None)),
        check_vma=False,
    )
```

```python
import functools

import jax
import jax.numpy as jnp
import numpy as np
from jax import lax
from jax.experimental import pallas as pl
from jax.experimental.pallas import tpu as pltpu
from jax.sharding import PartitionSpec as P

MESH = pl.DeviceIdType.MESH
NN = (((1,), (0,)), ((), ()))
NT = (((1,), (1,)), ((), ()))

highest = lax.Precision.HIGHEST
epsilon = 1e-05


def layer_norm(values):
    center = values - jnp.mean(values, axis=-1, keepdims=True)
    spread = jnp.mean(center * center, axis=-1, keepdims=True)
    return center * lax.rsqrt(spread + epsilon)


def matmul(left_side, right_side):
    return jnp.dot(left_side, right_side, precision=highest, preferred_element_type=jnp.float32)


def outer_block(left_rows, right_cols, outer_out):
    product = jnp.einsum("sip,sjq->ijpq", left_rows, right_cols, precision=highest)
    row_total, col_total, left_width, right_width = product.shape
    return matmul(product.reshape(row_total, col_total, left_width * right_width), outer_out)


def shards(
    pair_rep,
    alignment,
    residue_mask,
    row_mask,
    attention_in,
    pair_bias_w,
    attention_out,
    outer_in,
    outer_out,
    triangle_in,
    triangle_gate,
    triangle_out,
    transit_in,
    transit_out,
):
    row_count, col_count, _ = pair_rep.shape
    seq_count = alignment.shape[0]
    head_count = pair_bias_w.shape[1]
    att_width = attention_out.shape[0]
    head_depth = att_width // head_count
    outer_width = outer_in.shape[1] // 2
    inner_width = triangle_out.shape[0]
    row_start = lax.axis_index(("branch", "prow")) * row_count
    col_start = lax.axis_index("pcol") * col_count
    pair_norm = layer_norm(pair_rep)
    bias_tile = jnp.einsum("ijc,ch->hij", pair_norm, pair_bias_w, precision=highest)
    bias_rows = lax.all_gather(bias_tile, "pcol", axis=2, tiled=True)
    normed = layer_norm(alignment)
    mask_float = row_mask.astype(jnp.float32)
    key_bias = 1000000000.0 * (mask_float - 1.0)
    queries = matmul(normed, attention_in[:, :att_width]) * head_depth ** (-0.5)
    queries = queries.reshape(seq_count, row_count, head_count, head_depth)
    gate_logits = matmul(normed, attention_in[:, 3 * att_width :])
    key_value_w = attention_in[:, att_width : 3 * att_width]
    key_value_local = matmul(normed, key_value_w)
    widen = lambda sent_block: sent_block
    running_max = jnp.full((seq_count, head_count, row_count), -1e30, jnp.float32)
    make_sent_block = lax.all_gather(key_value_local, ("branch", "prow"), axis=1, tiled=True)
    block_bias = lax.all_gather(key_bias, ("branch", "prow"), axis=1, tiled=True)
    key_value = widen(make_sent_block)
    key_count = block_bias.shape[1]
    key_block = key_value[..., :att_width].reshape(seq_count, key_count, head_count, head_depth)
    value_block = key_value[..., att_width:].reshape(seq_count, key_count, head_count, head_depth)
    scores = jnp.einsum("sihd,sjhd->shij", queries, key_block, precision=highest)
    scores = scores + bias_rows[None] + block_bias[:, None, None, :]
    block_max = jnp.maximum(running_max, jnp.max(scores, axis=-1))
    weights = jnp.exp(scores - block_max[..., None])
    running_sum = jnp.sum(weights, axis=-1)
    accumulated = jnp.einsum("shij,sjhd->shid", weights, value_block, precision=highest)
    final_state = (block_max, running_sum, accumulated)
    _, running_sum, accumulated = final_state
    mixed = accumulated / running_sum[..., None]
    mixed = jnp.transpose(mixed, (0, 2, 1, 3)).reshape(seq_count, row_count, att_width)
    new_alignment = alignment + matmul(mixed * jax.nn.sigmoid(gate_logits), attention_out)
    factors = matmul(layer_norm(new_alignment), outer_in) * mask_float[..., None]
    left_outer = factors[..., :outer_width]
    right_outer = factors[..., outer_width:]
    right_all, mask_all = (
        lax.all_gather(right_outer, ("branch", "prow"), axis=1, tiled=True),
        lax.all_gather(mask_float, ("branch", "prow"), axis=1, tiled=True),
    )
    left_full, left_mask = (
        lax.all_gather(left_outer, "pcol", axis=0, tiled=True),
        lax.all_gather(mask_float, "pcol", axis=0, tiled=True),
    )
    right_tile, mask_tile = (
        lax.all_to_all(right_all, "pcol", split_axis=1, concat_axis=0, tiled=True),
        lax.all_to_all(mask_all, "pcol", split_axis=1, concat_axis=0, tiled=True),
    )
    outer_sum = outer_block(left_full, right_tile, outer_out)
    count_sum = jnp.einsum("si,sj->ij", left_mask, mask_tile, precision=highest)
    outer_mean = outer_sum / (1.0 + count_sum)[..., None]
    pair_one = pair_rep + outer_mean
    tri_norm = layer_norm(pair_one)
    res_float = residue_mask.astype(jnp.float32)
    row_valid = lax.dynamic_slice_in_dim(res_float, row_start, row_count)
    col_valid = lax.dynamic_slice_in_dim(res_float, col_start, col_count)
    pair_valid = (row_valid[:, None] * col_valid[None, :])[..., None]
    edges = matmul(tri_norm, triangle_in)
    left_edge = (
        jax.nn.sigmoid(edges[..., :inner_width])
        * edges[..., inner_width : 2 * inner_width]
        * pair_valid
    )
    right_edge = (
        jax.nn.sigmoid(edges[..., 2 * inner_width : 3 * inner_width])
        * edges[..., 3 * inner_width :]
        * pair_valid
    )
    cross_part = jnp.einsum(
        "ikc,jkc->ijc",
        left_edge,
        lax.all_gather(right_edge, ("branch", "prow"), axis=0, tiled=True),
        precision=highest,
    )
    crossed = lax.psum_scatter(cross_part, "pcol", scatter_dimension=1, tiled=True)
    triangle = matmul(layer_norm(crossed), triangle_out) * jax.nn.sigmoid(
        matmul(tri_norm, triangle_gate)
    )
    pair_mid = pair_one + triangle
    hidden_units = jax.nn.relu(matmul(layer_norm(pair_mid), transit_in))
    new_pair = pair_mid + matmul(hidden_units, transit_out)
    return (new_alignment, new_pair)


def split(values):
    high = values.astype(jnp.bfloat16)
    return high, (values - high.astype(jnp.float32)).astype(jnp.bfloat16)


def dot(a, b, dims=NN):
    return lax.dot_general(a, b, dims, preferred_element_type=jnp.float32)


def dot_split(a, b, dims=NN):
    return dot(a[0], b[0], dims) + (dot(a[0], b[1], dims) + dot(a[1], b[0], dims))


def mm(a, b, dims=NN):
    return dot_split(split(a), split(b), dims)


def mm_high(a, b, dims=NN):
    return lax.dot_general(a, b, dims, precision=highest, preferred_element_type=jnp.float32)


def sigmoid(v):
    return 1.0 / (1.0 + jnp.exp(-v))


def pick(matrix, pair, dims=NN):
    return tuple(dot(matrix, part, dims).astype(jnp.bfloat16) for part in pair)


def pick_right(pair, matrix):
    return tuple(dot(part, matrix).astype(jnp.bfloat16) for part in pair)


LOAD_ORDER = (0, 5, 1, 4, 3, 9, 15, 16, 2, 18, 6, 7, 8, 14, 10, 17, 11, 12, 13)


def block_kernel(sizes, count, *refs):
    hbm, outs, local = refs[:count], refs[count : count + 2], refs[count + 2 : 2 * count + 2]
    (
        pair_ref, ali_ref, res_ref, row_ref, ain_ref, pbw_ref, aout_ref, oin_ref, oout_ref,
        tin_ref, tgate_ref, tout_ref, xin_ref, xout_ref,
        perm_outer_ref, perm_gate_ref, perm_value_ref, perm_row_ref, pos_ref,
    ) = local
    nali_ref, npair_ref = outs
    (
        qsend, qrecv, bsend, brecv, msend, mrecv, frs, frr, fls, flr, es, er, cs, cr,
        lsc, tsc, p1, send_sem, recv_sem, load_sem,
    ) = refs[2 * count + 2 :]
    loads = [pltpu.make_async_copy(a, b, load_sem.at[n]) for n, (a, b) in enumerate(zip(hbm, local))]
    for n in LOAD_ORDER:
        loads[n].start()
    nb, np_, nc = sizes
    nr = nb * np_
    nd = nr * nc
    rb, cb, cz = pair_ref.shape
    sb, _, cm = ali_ref.shape
    seq = sb * nc
    res = rb * nr
    heads = pbw_ref.shape[0]
    att = aout_ref.shape[0]
    depth = att // heads
    groups = nr // sb
    hpg = heads // groups
    gw = hpg * depth
    ow = oin_ref.shape[0] // 2
    tri = tout_ref.shape[0]
    cpd = tri // nd
    per = nr // nc
    pos = rb * cb
    nib = pos // 128
    per_lane = 128 // cb
    order = [b * per_lane + n for n in range(per_lane) for b in range(nib)]
    brows = hpg * nib
    crows = cpd * nib
    f32 = jnp.float32

    r_me = lax.axis_index("branch") * np_ + lax.axis_index("prow")
    p_me = lax.axis_index("pcol")
    me = r_me * nc + p_me

    def where(r, p):
        return {"branch": r // np_, "prow": lax.rem(r, np_), "pcol": p}

    def al(v, m):
        return pl.multiple_of(v, m)

    def copy(phase, src, dst, tag, origin, r, p):
        return pltpu.make_async_remote_copy(
            src_ref=src, dst_ref=dst, send_sem=send_sem.at[phase, tag],
            recv_sem=recv_sem.at[phase, origin], device_id=where(r, p), device_id_type=MESH,
        )

    barrier = pltpu.get_barrier_semaphore()

    @pl.loop(1, nd)
    def _(k):
        t = lax.rem(me + k, nd)
        pl.semaphore_signal(barrier, inc=1, device_id=where(t // nc, lax.rem(t, nc)), device_id_type=MESH)

    loads[0].wait()
    loads[5].wait()
    pair = pair_ref[...].reshape(pos, cz)
    pair_norm = layer_norm(pair)
    bias_rows = mm_high(pbw_ref[...], pair_norm, NT)
    for b in range(nib):
        bsend[pl.ds(b, heads, stride=nib), :] = bias_rows[:, b * 128 : (b + 1) * 128]

    pl.semaphore_wait(barrier, nd - 1)

    def b_copy(r, p, origin_r, origin_p):
        group = lax.rem(r, groups)
        return copy(
            1, bsend.at[pl.ds(al(group * brows, brows), brows), :],
            brecv.at[origin_p, pl.ds(al(origin_r * brows, brows), brows), :],
            r * nc + p, origin_r * nc + origin_p, r, p,
        )

    @pl.loop(1, nd)
    def _(k):
        t = lax.rem(me + k, nd)
        b_copy(t // nc, lax.rem(t, nc), r_me, p_me).start()

    brecv[p_me, pl.ds(al(r_me * brows, brows), brows), :] = bsend[
        pl.ds(al(lax.rem(r_me, groups) * brows, brows), brows), :
    ]

    loads[1].wait()
    loads[4].wait()
    loads[3].wait()
    ali = ali_ref[...].reshape(sb * rb, cm)
    projected = mm(layer_norm(ali), ain_ref[...])
    gate = sigmoid(projected[:, 3 * att :])
    mask = row_ref[...].astype(f32)
    eye = (
        lax.broadcasted_iota(jnp.int32, (rb, rb), 0) == lax.broadcasted_iota(jnp.int32, (rb, rb), 1)
    ).astype(f32)
    mask_cols = [jnp.sum(eye * mask[s : s + 1, :], axis=1, keepdims=True) for s in range(sb)]
    for s in range(sb):
        rows = projected[s * rb : (s + 1) * rb]
        for g in range(groups):
            for n in range(3):
                qsend[s * groups + g, :, n * gw : (n + 1) * gw] = rows[
                    :, n * att + g * gw : n * att + (g + 1) * gw
                ]
            qsend[s * groups + g, :, 3 * gw :] = jnp.broadcast_to(mask_cols[s], (rb, gw))

    def q_copy(r, origin_r):
        return copy(
            0, qsend.at[r], qrecv.at[pl.ds(al(origin_r * rb, rb), rb), :], r, origin_r, r, p_me
        )

    @pl.loop(1, nr)
    def _(k):
        q_copy(lax.rem(r_me + k, nr), r_me).start()

    qrecv[pl.ds(al(r_me * rb, rb), rb), :] = qsend[r_me]

    loads[9].wait()
    loads[15].wait()
    loads[16].wait()
    loads[2].wait()
    loads[18].wait()
    tin = split(tin_ref[...])
    w_gate = pick(perm_gate_ref[...], tin, NT)
    w_value = pick(perm_value_ref[...], tin, NT)
    res_rows = jnp.broadcast_to(res_ref[...].astype(f32), (8, res)).astype(jnp.bfloat16)
    index = lax.broadcasted_iota(jnp.int32, (res, pos), 0)
    row_pick = (index == pos_ref[0:1, :] + r_me * rb).astype(jnp.bfloat16)
    col_pick = (index == pos_ref[1:2, :] + p_me * cb).astype(jnp.bfloat16)
    valid = (dot(res_rows, row_pick) * dot(res_rows, col_pick))[0:1, :]

    @pl.loop(1, nr)
    def _(k):
        q_copy(r_me, lax.rem(r_me + k, nr)).wait_recv()

    @pl.loop(1, nd)
    def _(k):
        t = lax.rem(me + k, nd)
        b_copy(r_me, p_me, t // nc, lax.rem(t, nc)).wait_recv()

    first = (lax.broadcasted_iota(jnp.int32, (8, gw), 1) == 0).astype(f32)
    mask_row = dot(first.astype(jnp.bfloat16), qrecv[:, 3 * gw :].astype(jnp.bfloat16), NT)[0:1]
    key_bias = 1000000000.0 * (mask_row - 1.0)
    msend[...] = qrecv[:, 0:128]
    query_rows = jnp.concatenate([msend[pl.ds(i, nr, stride=rb), :] for i in order], axis=0)
    mixed_heads = []
    for h in range(hpg):
        queries = query_rows[:, h * depth : (h + 1) * depth] * depth ** (-0.5)
        keys = qrecv[:, gw + h * depth : gw + (h + 1) * depth]
        vals = qrecv[:, 2 * gw + h * depth : 2 * gw + (h + 1) * depth]
        tiles = [
            [brecv[p, pl.ds(h * nib + b, nr, stride=brows), :] for p in range(nc)] for b in range(nib)
        ]
        bias = jnp.concatenate(
            [
                jnp.concatenate([half[:, n * cb : (n + 1) * cb] for half in tiles[b]], axis=1)
                for n in range(per_lane)
                for b in range(nib)
            ],
            axis=0,
        )
        scores = mm_high(queries, keys, NT) + bias + key_bias
        weights = jnp.exp(scores - jnp.max(scores, axis=1, keepdims=True))
        total = jnp.sum(weights, axis=1, keepdims=True)
        mixed_heads.append(mm(weights, vals) / total)
    mixed_heads.append(jnp.zeros((res, 128 - gw), f32))
    mixed_rows = jnp.concatenate(mixed_heads, axis=1)
    for n, i in enumerate(order):
        msend[pl.ds(i, nr, stride=rb), :] = mixed_rows[n * nr : (n + 1) * nr]

    def m_copy(r, origin_r):
        return copy(
            2, msend.at[pl.ds(al(r * rb, rb), rb), :], mrecv.at[origin_r], r, origin_r, r, p_me
        )

    @pl.loop(1, nr)
    def _(k):
        m_copy(lax.rem(r_me + k, nr), r_me).start()

    mrecv[r_me] = msend[pl.ds(al(r_me * rb, rb), rb), :]

    @pl.loop(1, nr)
    def _(k):
        m_copy(r_me, lax.rem(r_me + k, nr)).wait_recv()

    mixed = jnp.concatenate(
        [
            jnp.concatenate([mrecv[s * groups + g, :, :gw] for g in range(groups)], axis=1)
            for s in range(sb)
        ],
        axis=0,
    )
    loads[6].wait()
    loads[7].wait()
    new_ali = ali + mm(mixed * gate, aout_ref[...])
    factors = mm(layer_norm(new_ali), oin_ref[...], NT)
    width = sb * ow
    lane = lax.broadcasted_iota(jnp.int32, (rb, 128), 1)
    mask_lanes = jnp.zeros((rb, 128), f32)
    for s in range(sb):
        part = factors[s * rb : (s + 1) * rb] * mask_cols[s]
        fls[:, s * ow : (s + 1) * ow] = part[:, :ow]
        frs[:, s * ow : (s + 1) * ow] = part[:, ow:]
        mask_lanes = jnp.where(lane == s, mask_cols[s], mask_lanes)
    fls[:, width:] = mask_lanes
    frs[:, width:] = mask_lanes
    home = r_me // per

    def fr_copy(r, p, origin_r, origin_p):
        return copy(
            3, frs, frr.at[origin_p, pl.ds(al(lax.rem(origin_r, per) * rb, rb), rb), :],
            r, origin_r * nc + origin_p, r, p,
        )

    def fl_copy(p, origin_p):
        return copy(4, fls, flr.at[origin_p], p, origin_p, r_me, p)

    @pl.loop(0, nr)
    def _(k):
        r = lax.rem(r_me + k, nr)

        @pl.when(jnp.logical_or(r != r_me, home != p_me))
        def _():
            fr_copy(r, home, r_me, p_me).start()

    for k in range(1, nc):
        fl_copy(lax.rem(p_me + k, nc), p_me).start()

    nali_ref[...] = new_ali.reshape(sb, rb, cm)

    @pl.when(home == p_me)
    def _():
        frr[p_me, pl.ds(al(lax.rem(r_me, per) * rb, rb), rb), :] = frs[...]

    flr[p_me] = fls[...]

    for k in range(1, nc):
        fl_copy(p_me, lax.rem(p_me + k, nc)).wait_recv()

    for p in range(nc):
        for s in range(sb):
            lsc[pl.ds(p * sb + s, rb, stride=seq), :] = jnp.concatenate(
                [flr[p, :, s * ow : (s + 1) * ow], jnp.zeros((rb, 128 - ow), f32)], axis=1
            )
    left = lsc[:, :ow]
    left_high, left_low = split(left)
    left_cat = jnp.concatenate([left_high, left_low, left_high], axis=1)
    loads[8].wait()
    for q in range(ow):
        w_high, w_low = split(oout_ref[pl.ds(q, ow, stride=ow), :])
        w_cat = jnp.concatenate([w_high, w_high, w_low], axis=0)
        tsc[:, q, :, :] = dot(left_cat, w_cat).reshape(rb, seq, cz)

    @pl.loop(0, per * nc)
    def _(k):
        origin_r = p_me * per + k // nc
        origin_p = lax.rem(k, nc)

        @pl.when(jnp.logical_or(origin_r != r_me, origin_p != p_me))
        def _():
            fr_copy(r_me, p_me, origin_r, origin_p).wait_recv()

    loads[14].wait()
    right = pick_right(
        split(jnp.concatenate([frr[p, :, :width] for p in range(nc)], axis=1)), perm_outer_ref[...]
    )
    mask_right = jnp.concatenate([frr[p, :, width : width + sb] for p in range(nc)], axis=1)
    mask_left = jnp.concatenate([flr[p, :, width : width + sb] for p in range(nc)], axis=1)
    for i in range(rb):
        outer = dot_split(right, split(tsc[i].reshape(ow * seq, cz)))
        count = jnp.sum(mask_right * mask_left[i : i + 1, :], axis=1, keepdims=True)
        p1[i * cb : (i + 1) * cb, :] = pair_ref[i] + outer / (1.0 + count)
    pair_one = p1[...]
    tri_norm = layer_norm(pair_one)
    tri_split = split(tri_norm)
    edge = sigmoid(dot_split(w_gate, tri_split, NT)) * dot_split(w_value, tri_split, NT) * valid
    for b in range(nib):
        es[b] = edge[:, b * 128 : (b + 1) * 128]

    rows_each = 2 * cpd

    def e_copy(r, p, origin_r, origin_p):
        return copy(
            5, es.at[:, pl.ds(al((r * nc + p) * rows_each, rows_each), rows_each), :],
            er.at[:, pl.ds(al((origin_p * nr + origin_r) * rows_each, rows_each), rows_each), :],
            r * nc + p, origin_r * nc + origin_p, r, p,
        )

    @pl.loop(1, nd)
    def _(k):
        t = lax.rem(me + k, nd)
        e_copy(t // nc, lax.rem(t, nc), r_me, p_me).start()

    er[:, pl.ds(al((p_me * nr + r_me) * rows_each, rows_each), rows_each), :] = es[
        :, pl.ds(al(me * rows_each, rows_each), rows_each), :
    ]
    loads[10].wait()
    loads[17].wait()
    loads[11].wait()
    loads[12].wait()
    loads[13].wait()
    out_gate = sigmoid(dot_split(tri_split, split(tgate_ref[...])))

    @pl.loop(1, nd)
    def _(k):
        t = lax.rem(me + k, nd)
        e_copy(r_me, p_me, t // nc, lax.rem(t, nc)).wait_recv()

    def edge_blocks(row):
        blocks = []
        for b in range(nib):
            halves = [er[b, pl.ds(p * nr * rows_each + row, nr, stride=rows_each), :] for p in range(nc)]
            for n in range(per_lane):
                blocks.append(
                    jnp.concatenate([half[:, n * cb : (n + 1) * cb] for half in halves], axis=1)
                )
        return blocks

    for c in range(cpd):
        blocks = edge_blocks(c)
        left_rows = split(jnp.concatenate([blocks[i] for i in order], axis=0))
        right_rows = pick(perm_row_ref[...], split(jnp.concatenate(edge_blocks(cpd + c), axis=0)))
        crossed = dot_split(left_rows, right_rows, NT)
        for p in range(nc):
            half = crossed[:, p * cb : (p + 1) * cb]
            packed = jnp.concatenate(
                [half[n * nib * nr : (n + 1) * nib * nr] for n in range(per_lane)], axis=1
            )
            for b in range(nib):
                cs[p, pl.ds(c * nib + b, nr, stride=crows), :] = packed[b * nr : (b + 1) * nr]

    def c_copy(r, p, origin):
        return copy(
            6, cs.at[p, pl.ds(al(r * crows, crows), crows), :],
            cr.at[pl.ds(al(origin * crows, crows), crows), :],
            r * nc + p, origin, r, p,
        )

    @pl.loop(1, nd)
    def _(k):
        t = lax.rem(me + k, nd)
        c_copy(t // nc, lax.rem(t, nc), me).start()

    cr[pl.ds(al(me * crows, crows), crows), :] = cs[p_me, pl.ds(al(r_me * crows, crows), crows), :]

    @pl.loop(1, nd)
    def _(k):
        t = lax.rem(me + k, nd)
        c_copy(r_me, p_me, t).wait_recv()

    w_out = split(tout_ref[...])
    tri_rows = []
    for b in range(nib):
        channels = cr[pl.ds(b, tri, stride=nib), :]
        tri_rows.append(dot_split(split(layer_norm(channels.T)), w_out))
    triangle = jnp.concatenate(tri_rows, axis=0) * out_gate
    pair_mid = pair_one + triangle
    hidden = jnp.maximum(mm(layer_norm(pair_mid), xin_ref[...]), 0.0)
    npair_ref[...] = (pair_mid + mm(hidden, xout_ref[...])).reshape(rb, cb, cz)

    @pl.loop(1, nr)
    def _(k):
        r = lax.rem(r_me + k, nr)
        q_copy(r, r_me).wait_send()
        m_copy(r, r_me).wait_send()

    @pl.loop(0, nr)
    def _(k):
        r = lax.rem(r_me + k, nr)

        @pl.when(jnp.logical_or(r != r_me, home != p_me))
        def _():
            fr_copy(r, home, r_me, p_me).wait_send()

    for k in range(1, nc):
        fl_copy(lax.rem(p_me + k, nc), p_me).wait_send()

    @pl.loop(1, nd)
    def _(k):
        t = lax.rem(me + k, nd)
        b_copy(t // nc, lax.rem(t, nc), r_me, p_me).wait_send()
        e_copy(t // nc, lax.rem(t, nc), r_me, p_me).wait_send()
        c_copy(t // nc, lax.rem(t, nc), me).wait_send()


def fused(sizes, *args):
    (pair, ali, res_mask, row_mask, ain, pbw, aout, oin, oout, tin, tgate, tout, xin, xout) = args
    nb, np_, nc = sizes
    nr = nb * np_
    nd = nr * nc
    rb, cb, cz = pair.shape
    sb, _, cm = ali.shape
    res = rb * nr
    seq = sb * nc
    heads = pbw.shape[1]
    depth = aout.shape[0] // heads
    groups = nr // sb
    hpg = heads // groups
    gw = hpg * depth
    ow = oin.shape[1] // 2
    tri = tout.shape[0]
    cpd = tri // nd
    pos = rb * cb
    nib = pos // 128
    f32 = jnp.float32

    a = np.arange(seq * ow)
    perm_outer = np.zeros((seq * ow, seq * ow), np.float32)
    perm_outer[a, (a % ow) * seq + a // ow] = 1.0
    row = np.arange(2 * tri)
    channel = (row // cpd % 2) * 2 * tri + (row // (2 * cpd)) * cpd + row % cpd
    perm_gate = np.zeros((2 * tri, 4 * tri), np.float32)
    perm_gate[row, channel] = 1.0
    perm_value = np.zeros((2 * tri, 4 * tri), np.float32)
    perm_value[row, channel + tri] = 1.0
    n = np.arange(res)
    perm_row = np.zeros((res, res), np.float32)
    perm_row[n, (n % rb) * nr + n // rb] = 1.0
    position = np.arange(pos)
    pos_table = np.stack([position // cb, position % cb]).astype(np.int32)
    consts = [jnp.asarray(m, jnp.bfloat16) for m in (perm_outer, perm_gate, perm_value, perm_row)]
    operands = [
        pair, ali, res_mask.reshape(1, res), row_mask, ain, pbw.T, aout, oin.T, oout, tin, tgate, tout,
        xin, xout, *consts, jnp.asarray(pos_table),
    ]
    vmem = pl.BlockSpec(memory_space=pltpu.VMEM)
    fw = sb * ow + 128
    scratch = [
        ((nr, rb, 4 * gw)), ((res, 4 * gw)),
        ((heads * nib, 128)), ((nc, nr * hpg * nib, 128)),
        ((res, 128)), ((nr, rb, 128)),
        ((rb, fw)), ((nc, cb, fw)), ((rb, fw)), ((nc, rb, fw)),
        ((pos // 128, 2 * tri, 128)), ((pos // 128, 2 * tri, 128)),
        ((nc, nr * cpd * nib, 128)), ((tri * nib, 128)),
        ((rb * seq, 128)), ((rb, ow, seq, cz)), ((pos, cz)),
    ]
    return pl.pallas_call(
        functools.partial(block_kernel, sizes, len(operands)),
        out_shape=(
            jax.ShapeDtypeStruct(ali.shape, f32),
            jax.ShapeDtypeStruct(pair.shape, f32),
        ),
        in_specs=[pl.BlockSpec(memory_space=pltpu.HBM)] * len(operands),
        out_specs=(vmem, vmem),
        scratch_shapes=[pltpu.VMEM(m.shape, m.dtype) for m in operands]
        + [pltpu.VMEM(s, f32) for s in scratch]
        + [pltpu.SemaphoreType.DMA((7, nd)), pltpu.SemaphoreType.DMA((7, nd))]
        + [pltpu.SemaphoreType.DMA((len(operands),))],
        compiler_params=pltpu.CompilerParams(
            collective_id=0, has_side_effects=True, vmem_limit_bytes=63 * 1024 * 1024
        ),
    )(*operands)


def fits(sizes, args):
    pair, ali, pbw, aout, oin, tout = (args[n] for n in (0, 1, 5, 6, 7, 11))
    nb, np_, nc = sizes
    nr = nb * np_
    rb, cb, cz = pair.shape
    sb = ali.shape[0]
    heads = pbw.shape[1]
    depth = aout.shape[0] // heads
    if nr % sb or heads % (nr // sb) or nr % nc or tout.shape[0] % (nr * nc):
        return False
    return (
        ali.shape[1] == rb and rb % 8 == 0 and cb * nc == rb * nr and 128 % cb == 0 and cz == 128
        and (sb * nc) % 8 == 0 and (2 * (tout.shape[0] // (nr * nc))) % 8 == 0
        and (heads // (nr // sb)) * depth * 4 % 128 == 0 and sb * (oin.shape[1] // 2) % 128 == 0
        and rb % (128 // cb) == 0 and (heads // (nr // sb)) * depth * 2 == 128
        and (heads // (nr // sb)) * (rb * cb // 128) % 8 == 0
        and tout.shape[0] // (nr * nc) * (rb * cb // 128) % 8 == 0
    )


def solution(mesh):
    sizes = tuple(mesh.shape[name] for name in ("branch", "prow", "pcol"))

    def local(*args):
        if fits(sizes, args):
            return fused(sizes, *args)
        return shards(*args)

    return jax.shard_map(
        local,
        mesh=mesh,
        in_specs=(
            P(("branch", "prow"), "pcol", None),
            P("pcol", ("branch", "prow"), None),
            P(),
            P("pcol", ("branch", "prow")),
            P(),
            P(),
            P(),
            P(),
            P(),
            P(),
            P(),
            P(),
            P(),
            P(),
        ),
        out_specs=(P("pcol", ("branch", "prow"), None), P(("branch", "prow"), "pcol", None)),
        check_vma=False,
    )
```

```python
import functools

import jax
import jax.numpy as jnp
import numpy as np
from jax import lax
from jax.experimental import pallas as pl
from jax.experimental.pallas import tpu as pltpu
from jax.sharding import PartitionSpec as P

MESH = pl.DeviceIdType.MESH
NN = (((1,), (0,)), ((), ()))
NT = (((1,), (1,)), ((), ()))

highest = lax.Precision.HIGHEST
epsilon = 1e-05


def layer_norm(values):
    center = values - jnp.mean(values, axis=-1, keepdims=True)
    spread = jnp.mean(center * center, axis=-1, keepdims=True)
    return center * lax.rsqrt(spread + epsilon)


def matmul(left_side, right_side):
    return jnp.dot(left_side, right_side, precision=highest, preferred_element_type=jnp.float32)


def outer_block(left_rows, right_cols, outer_out):
    product = jnp.einsum("sip,sjq->ijpq", left_rows, right_cols, precision=highest)
    row_total, col_total, left_width, right_width = product.shape
    return matmul(product.reshape(row_total, col_total, left_width * right_width), outer_out)


def shards(
    pair_rep,
    alignment,
    residue_mask,
    row_mask,
    attention_in,
    pair_bias_w,
    attention_out,
    outer_in,
    outer_out,
    triangle_in,
    triangle_gate,
    triangle_out,
    transit_in,
    transit_out,
):
    row_count, col_count, _ = pair_rep.shape
    seq_count = alignment.shape[0]
    head_count = pair_bias_w.shape[1]
    att_width = attention_out.shape[0]
    head_depth = att_width // head_count
    outer_width = outer_in.shape[1] // 2
    inner_width = triangle_out.shape[0]
    row_start = lax.axis_index(("branch", "prow")) * row_count
    col_start = lax.axis_index("pcol") * col_count
    pair_norm = layer_norm(pair_rep)
    bias_tile = jnp.einsum("ijc,ch->hij", pair_norm, pair_bias_w, precision=highest)
    bias_rows = lax.all_gather(bias_tile, "pcol", axis=2, tiled=True)
    normed = layer_norm(alignment)
    mask_float = row_mask.astype(jnp.float32)
    key_bias = 1000000000.0 * (mask_float - 1.0)
    queries = matmul(normed, attention_in[:, :att_width]) * head_depth ** (-0.5)
    queries = queries.reshape(seq_count, row_count, head_count, head_depth)
    gate_logits = matmul(normed, attention_in[:, 3 * att_width :])
    key_value_w = attention_in[:, att_width : 3 * att_width]
    key_value_local = matmul(normed, key_value_w)
    widen = lambda sent_block: sent_block
    running_max = jnp.full((seq_count, head_count, row_count), -1e30, jnp.float32)
    make_sent_block = lax.all_gather(key_value_local, ("branch", "prow"), axis=1, tiled=True)
    block_bias = lax.all_gather(key_bias, ("branch", "prow"), axis=1, tiled=True)
    key_value = widen(make_sent_block)
    key_count = block_bias.shape[1]
    key_block = key_value[..., :att_width].reshape(seq_count, key_count, head_count, head_depth)
    value_block = key_value[..., att_width:].reshape(seq_count, key_count, head_count, head_depth)
    scores = jnp.einsum("sihd,sjhd->shij", queries, key_block, precision=highest)
    scores = scores + bias_rows[None] + block_bias[:, None, None, :]
    block_max = jnp.maximum(running_max, jnp.max(scores, axis=-1))
    weights = jnp.exp(scores - block_max[..., None])
    running_sum = jnp.sum(weights, axis=-1)
    accumulated = jnp.einsum("shij,sjhd->shid", weights, value_block, precision=highest)
    final_state = (block_max, running_sum, accumulated)
    _, running_sum, accumulated = final_state
    mixed = accumulated / running_sum[..., None]
    mixed = jnp.transpose(mixed, (0, 2, 1, 3)).reshape(seq_count, row_count, att_width)
    new_alignment = alignment + matmul(mixed * jax.nn.sigmoid(gate_logits), attention_out)
    factors = matmul(layer_norm(new_alignment), outer_in) * mask_float[..., None]
    left_outer = factors[..., :outer_width]
    right_outer = factors[..., outer_width:]
    right_all, mask_all = (
        lax.all_gather(right_outer, ("branch", "prow"), axis=1, tiled=True),
        lax.all_gather(mask_float, ("branch", "prow"), axis=1, tiled=True),
    )
    left_full, left_mask = (
        lax.all_gather(left_outer, "pcol", axis=0, tiled=True),
        lax.all_gather(mask_float, "pcol", axis=0, tiled=True),
    )
    right_tile, mask_tile = (
        lax.all_to_all(right_all, "pcol", split_axis=1, concat_axis=0, tiled=True),
        lax.all_to_all(mask_all, "pcol", split_axis=1, concat_axis=0, tiled=True),
    )
    outer_sum = outer_block(left_full, right_tile, outer_out)
    count_sum = jnp.einsum("si,sj->ij", left_mask, mask_tile, precision=highest)
    outer_mean = outer_sum / (1.0 + count_sum)[..., None]
    pair_one = pair_rep + outer_mean
    tri_norm = layer_norm(pair_one)
    res_float = residue_mask.astype(jnp.float32)
    row_valid = lax.dynamic_slice_in_dim(res_float, row_start, row_count)
    col_valid = lax.dynamic_slice_in_dim(res_float, col_start, col_count)
    pair_valid = (row_valid[:, None] * col_valid[None, :])[..., None]
    edges = matmul(tri_norm, triangle_in)
    left_edge = (
        jax.nn.sigmoid(edges[..., :inner_width])
        * edges[..., inner_width : 2 * inner_width]
        * pair_valid
    )
    right_edge = (
        jax.nn.sigmoid(edges[..., 2 * inner_width : 3 * inner_width])
        * edges[..., 3 * inner_width :]
        * pair_valid
    )
    cross_part = jnp.einsum(
        "ikc,jkc->ijc",
        left_edge,
        lax.all_gather(right_edge, ("branch", "prow"), axis=0, tiled=True),
        precision=highest,
    )
    crossed = lax.psum_scatter(cross_part, "pcol", scatter_dimension=1, tiled=True)
    triangle = matmul(layer_norm(crossed), triangle_out) * jax.nn.sigmoid(
        matmul(tri_norm, triangle_gate)
    )
    pair_mid = pair_one + triangle
    hidden_units = jax.nn.relu(matmul(layer_norm(pair_mid), transit_in))
    new_pair = pair_mid + matmul(hidden_units, transit_out)
    return (new_alignment, new_pair)


def split(values):
    high = values.astype(jnp.bfloat16)
    return high, (values - high.astype(jnp.float32)).astype(jnp.bfloat16)


def dot(a, b, dims=NN):
    return lax.dot_general(a, b, dims, preferred_element_type=jnp.float32)


def dot_split(a, b, dims=NN):
    rows, depth = a[0].shape
    if rows <= 64:
        both = dot(jnp.concatenate(a, axis=0), b[0], dims)
        return both[:rows] + (both[rows:] + dot(a[0], b[1], dims))
    if depth == 128:
        axis = dims[0][1][0]
        twice = dot(jnp.concatenate(a, axis=1), jnp.concatenate([b[0], b[0]], axis=axis), dims)
        return twice + dot(a[0], b[1], dims)
    return dot(a[0], b[0], dims) + (dot(a[0], b[1], dims) + dot(a[1], b[0], dims))


def mm(a, b, dims=NN):
    return dot_split(split(a), split(b), dims)


def mm_high(a, b, dims=NN):
    return lax.dot_general(a, b, dims, precision=highest, preferred_element_type=jnp.float32)


def sigmoid(v):
    return 1.0 / (1.0 + jnp.exp(-v))


def pick(matrix, pair, dims=NN):
    return tuple(dot(matrix, part, dims).astype(jnp.bfloat16) for part in pair)


def pick_right(pair, matrix):
    return tuple(dot(part, matrix).astype(jnp.bfloat16) for part in pair)


EDGE_CHUNKS = 1
CROSS_CHUNKS = 1
LOAD_ORDER = (0, 5, 1, 4, 3, 9, 15, 16, 2, 18, 6, 7, 8, 14, 10, 17, 11, 12, 13)


def block_kernel(sizes, count, *refs):
    hbm, outs, local = refs[:count], refs[count : count + 2], refs[count + 2 : 2 * count + 2]
    (
        pair_ref, ali_ref, res_ref, row_ref, ain_ref, pbw_ref, aout_ref, oin_ref, oout_ref,
        tin_ref, tgate_ref, tout_ref, xin_ref, xout_ref,
        perm_outer_ref, perm_gate_ref, perm_value_ref, perm_row_ref, pos_ref,
    ) = local
    nali_ref, npair_ref = outs
    (
        qsend, qrecv, bsend, brecv, msend, mrecv, frs, frr, fls, flr, es, er, cs, cr,
        lsc, tsc, p1, wcat, send_sem, recv_sem, load_sem,
    ) = refs[2 * count + 2 :]
    loads = [pltpu.make_async_copy(a, b, load_sem.at[n]) for n, (a, b) in enumerate(zip(hbm, local))]
    for n in LOAD_ORDER:
        loads[n].start()
    nb, np_, nc = sizes
    nr = nb * np_
    nd = nr * nc
    rb, cb, cz = pair_ref.shape
    sb, _, cm = ali_ref.shape
    seq = sb * nc
    res = rb * nr
    heads = pbw_ref.shape[0]
    att = aout_ref.shape[0]
    depth = att // heads
    groups = nr // sb
    hpg = heads // groups
    gw = hpg * depth
    ow = oin_ref.shape[0] // 2
    tri = tout_ref.shape[0]
    cpd = tri // nd
    per = nr // nc
    pos = rb * cb
    nib = pos // 128
    per_lane = 128 // cb
    order = [b * per_lane + n for n in range(per_lane) for b in range(nib)]
    brows = hpg * nib
    crows = cpd * nib
    f32 = jnp.float32

    r_me = lax.axis_index("branch") * np_ + lax.axis_index("prow")
    p_me = lax.axis_index("pcol")
    me = r_me * nc + p_me

    def where(r, p):
        return {"branch": r // np_, "prow": lax.rem(r, np_), "pcol": p}

    def al(v, m):
        return pl.multiple_of(v, m)

    def copy(phase, src, dst, tag, origin, r, p):
        return pltpu.make_async_remote_copy(
            src_ref=src, dst_ref=dst, send_sem=send_sem.at[phase, tag],
            recv_sem=recv_sem.at[phase, origin], device_id=where(r, p), device_id_type=MESH,
        )

    barrier = pltpu.get_barrier_semaphore()

    @pl.loop(1, nd)
    def _(k):
        t = lax.rem(me + k, nd)
        pl.semaphore_signal(barrier, inc=1, device_id=where(t // nc, lax.rem(t, nc)), device_id_type=MESH)

    loads[0].wait()
    loads[5].wait()
    pair = pair_ref[...].reshape(pos, cz)
    pair_norm = layer_norm(pair)
    bias_rows = mm_high(pbw_ref[...], pair_norm, NT)
    for b in range(nib):
        bsend[pl.ds(b, heads, stride=nib), :] = bias_rows[:, b * 128 : (b + 1) * 128]

    pl.semaphore_wait(barrier, nd - 1)

    def b_copy(r, p, origin_r, origin_p):
        group = lax.rem(r, groups)
        return copy(
            1, bsend.at[pl.ds(al(group * brows, brows), brows), :],
            brecv.at[origin_p, pl.ds(al(origin_r * brows, brows), brows), :],
            r * nc + p, origin_r * nc + origin_p, r, p,
        )

    @pl.loop(1, nd)
    def _(k):
        t = lax.rem(me + k, nd)
        b_copy(t // nc, lax.rem(t, nc), r_me, p_me).start()

    brecv[p_me, pl.ds(al(r_me * brows, brows), brows), :] = bsend[
        pl.ds(al(lax.rem(r_me, groups) * brows, brows), brows), :
    ]

    loads[1].wait()
    loads[4].wait()
    loads[3].wait()
    ali = ali_ref[...].reshape(sb * rb, cm)
    projected = mm(layer_norm(ali), ain_ref[...])
    gate = sigmoid(projected[:, 3 * att :])
    mask = row_ref[...].astype(f32)
    eye = (
        lax.broadcasted_iota(jnp.int32, (rb, rb), 0) == lax.broadcasted_iota(jnp.int32, (rb, rb), 1)
    ).astype(f32)
    mask_cols = [jnp.sum(eye * mask[s : s + 1, :], axis=1, keepdims=True) for s in range(sb)]
    for s in range(sb):
        rows = projected[s * rb : (s + 1) * rb]
        for g in range(groups):
            for n in range(3):
                qsend[s * groups + g, :, n * gw : (n + 1) * gw] = rows[
                    :, n * att + g * gw : n * att + (g + 1) * gw
                ]
            qsend[s * groups + g, :, 3 * gw :] = jnp.broadcast_to(mask_cols[s], (rb, gw))

    def q_copy(r, origin_r):
        return copy(
            0, qsend.at[r], qrecv.at[pl.ds(al(origin_r * rb, rb), rb), :], r, origin_r, r, p_me
        )

    @pl.loop(1, nr)
    def _(k):
        q_copy(lax.rem(r_me + k, nr), r_me).start()

    qrecv[pl.ds(al(r_me * rb, rb), rb), :] = qsend[r_me]

    loads[9].wait()
    loads[15].wait()
    loads[16].wait()
    loads[2].wait()
    loads[18].wait()
    tin = split(tin_ref[...])
    w_gate = pick(perm_gate_ref[...], tin, NT)
    w_value = pick(perm_value_ref[...], tin, NT)
    w_edges = tuple(jnp.concatenate(half, axis=0) for half in zip(w_gate, w_value))
    res_rows = jnp.broadcast_to(res_ref[...].astype(f32), (8, res)).astype(jnp.bfloat16)
    index = lax.broadcasted_iota(jnp.int32, (res, pos), 0)
    row_pick = (index == pos_ref[0:1, :] + r_me * rb).astype(jnp.bfloat16)
    col_pick = (index == pos_ref[1:2, :] + p_me * cb).astype(jnp.bfloat16)
    valid = (dot(res_rows, row_pick) * dot(res_rows, col_pick))[0:1, :]

    loads[6].wait()
    loads[7].wait()
    loads[8].wait()
    w_att = split(aout_ref[...])
    w_factor = split(oin_ref[...])
    for q in range(ow):
        w_high, w_low = split(oout_ref[pl.ds(q, ow, stride=ow), :])
        wcat[q] = jnp.concatenate([w_high, w_high, w_low], axis=0)

    @pl.loop(1, nr)
    def _(k):
        q_copy(r_me, lax.rem(r_me + k, nr)).wait_recv()

    @pl.loop(1, nd)
    def _(k):
        t = lax.rem(me + k, nd)
        b_copy(r_me, p_me, t // nc, lax.rem(t, nc)).wait_recv()

    first = (lax.broadcasted_iota(jnp.int32, (8, gw), 1) == 0).astype(f32)
    mask_row = dot(first.astype(jnp.bfloat16), qrecv[:, 3 * gw :].astype(jnp.bfloat16), NT)[0:1]
    key_bias = 1000000000.0 * (mask_row - 1.0)
    msend[...] = qrecv[:, 0:128]
    query_rows = jnp.concatenate([msend[pl.ds(i, nr, stride=rb), :] for i in order], axis=0)
    mixed_heads = []
    for h in range(hpg):
        queries = query_rows[:, h * depth : (h + 1) * depth] * depth ** (-0.5)
        keys = qrecv[:, gw + h * depth : gw + (h + 1) * depth]
        vals = qrecv[:, 2 * gw + h * depth : 2 * gw + (h + 1) * depth]
        tiles = [
            [brecv[p, pl.ds(h * nib + b, nr, stride=brows), :] for p in range(nc)] for b in range(nib)
        ]
        bias = jnp.concatenate(
            [
                jnp.concatenate([half[:, n * cb : (n + 1) * cb] for half in tiles[b]], axis=1)
                for n in range(per_lane)
                for b in range(nib)
            ],
            axis=0,
        )
        scores = mm_high(queries, keys, NT) + bias + key_bias
        weights = jnp.exp(scores - jnp.max(scores, axis=1, keepdims=True))
        total = jnp.sum(weights, axis=1, keepdims=True)
        mixed_heads.append(mm(weights, vals) / total)
    mixed_heads.append(jnp.zeros((res, 128 - gw), f32))
    mixed_rows = jnp.concatenate(mixed_heads, axis=1)
    for n, i in enumerate(order):
        msend[pl.ds(i, nr, stride=rb), :] = mixed_rows[n * nr : (n + 1) * nr]

    def m_copy(r, origin_r):
        return copy(
            2, msend.at[pl.ds(al(r * rb, rb), rb), :], mrecv.at[origin_r], r, origin_r, r, p_me
        )

    @pl.loop(1, nr)
    def _(k):
        m_copy(lax.rem(r_me + k, nr), r_me).start()

    mrecv[r_me] = msend[pl.ds(al(r_me * rb, rb), rb), :]

    @pl.loop(1, nr)
    def _(k):
        m_copy(r_me, lax.rem(r_me + k, nr)).wait_recv()

    mixed = jnp.concatenate(
        [
            jnp.concatenate([mrecv[s * groups + g, :, :gw] for g in range(groups)], axis=1)
            for s in range(sb)
        ],
        axis=0,
    )
    new_ali = ali + dot_split(split(mixed * gate), w_att)
    factors = dot_split(split(layer_norm(new_ali)), w_factor, NT)
    width = sb * ow
    lane = lax.broadcasted_iota(jnp.int32, (rb, 128), 1)
    mask_lanes = jnp.zeros((rb, 128), f32)
    for s in range(sb):
        part = factors[s * rb : (s + 1) * rb] * mask_cols[s]
        fls[:, s * ow : (s + 1) * ow] = part[:, :ow]
        frs[:, s * ow : (s + 1) * ow] = part[:, ow:]
        mask_lanes = jnp.where(lane == s, mask_cols[s], mask_lanes)
    fls[:, width:] = mask_lanes
    frs[:, width:] = mask_lanes
    home = r_me // per

    def fr_copy(r, p, origin_r, origin_p):
        return copy(
            3, frs, frr.at[origin_p, pl.ds(al(lax.rem(origin_r, per) * rb, rb), rb), :],
            r, origin_r * nc + origin_p, r, p,
        )

    def fl_copy(p, origin_p):
        return copy(4, fls, flr.at[origin_p], p, origin_p, r_me, p)

    @pl.loop(0, nr)
    def _(k):
        r = lax.rem(r_me + k, nr)

        @pl.when(jnp.logical_or(r != r_me, home != p_me))
        def _():
            fr_copy(r, home, r_me, p_me).start()

    for k in range(1, nc):
        fl_copy(lax.rem(p_me + k, nc), p_me).start()

    nali_ref[...] = new_ali.reshape(sb, rb, cm)

    @pl.when(home == p_me)
    def _():
        frr[p_me, pl.ds(al(lax.rem(r_me, per) * rb, rb), rb), :] = frs[...]

    flr[p_me] = fls[...]

    for k in range(1, nc):
        fl_copy(p_me, lax.rem(p_me + k, nc)).wait_recv()

    for p in range(nc):
        for s in range(sb):
            lsc[pl.ds(p * sb + s, rb, stride=seq), :] = jnp.concatenate(
                [flr[p, :, s * ow : (s + 1) * ow], jnp.zeros((rb, 128 - ow), f32)], axis=1
            )
    left = lsc[:, :ow]
    left_high, left_low = split(left)
    left_cat = jnp.concatenate([left_high, left_low, left_high], axis=1)
    for q in range(ow):
        tsc[:, q, :, :] = dot(left_cat, wcat[q]).reshape(rb, seq, cz)

    @pl.loop(0, per * nc)
    def _(k):
        origin_r = p_me * per + k // nc
        origin_p = lax.rem(k, nc)

        @pl.when(jnp.logical_or(origin_r != r_me, origin_p != p_me))
        def _():
            fr_copy(r_me, p_me, origin_r, origin_p).wait_recv()

    loads[14].wait()
    right = pick_right(
        split(jnp.concatenate([frr[p, :, :width] for p in range(nc)], axis=1)), perm_outer_ref[...]
    )
    mask_right = jnp.concatenate([frr[p, :, width : width + sb] for p in range(nc)], axis=1)
    mask_left = jnp.concatenate([flr[p, :, width : width + sb] for p in range(nc)], axis=1)
    rows_each = 2 * cpd
    step = nib // EDGE_CHUNKS

    def e_copy(chunk, r, p, origin_r, origin_p):
        return copy(
            5 + chunk,
            es.at[pl.ds(chunk * step, step), pl.ds(al((r * nc + p) * rows_each, rows_each), rows_each), :],
            er.at[
                pl.ds(chunk * step, step),
                pl.ds(al((origin_p * nr + origin_r) * rows_each, rows_each), rows_each), :,
            ],
            r * nc + p, origin_r * nc + origin_p, r, p,
        )

    def e_send(chunk):
        @pl.loop(1, nd)
        def _(k):
            t = lax.rem(me + k, nd)
            e_copy(chunk, t // nc, lax.rem(t, nc), r_me, p_me).start()

    for chunk in range(EDGE_CHUNKS):
        begin, end = chunk * step * 128, (chunk + 1) * step * 128
        for i in range(begin // cb, end // cb):
            outer = dot_split(right, split(tsc[i].reshape(ow * seq, cz)))
            count = jnp.sum(mask_right * mask_left[i : i + 1, :], axis=1, keepdims=True)
            p1[i * cb : (i + 1) * cb, :] = pair_ref[i] + outer / (1.0 + count)
        part = split(layer_norm(p1[begin:end, :]))
        raw = dot_split(w_edges, part, NT)
        edge = sigmoid(raw[: 2 * tri]) * raw[2 * tri :]
        edge = edge * valid[:, begin:end]
        for b in range(step):
            es[chunk * step + b] = edge[:, b * 128 : (b + 1) * 128]
        e_send(chunk)

    er[:, pl.ds(al((p_me * nr + r_me) * rows_each, rows_each), rows_each), :] = es[
        :, pl.ds(al(me * rows_each, rows_each), rows_each), :
    ]
    loads[10].wait()
    loads[17].wait()
    loads[11].wait()
    loads[12].wait()
    loads[13].wait()
    pair_one = p1[...]
    out_gate = sigmoid(dot_split(split(layer_norm(pair_one)), split(tgate_ref[...])))
    w_out = split(tout_ref[...])
    w_in = split(xin_ref[...])
    w_back = split(xout_ref[...])

    @pl.loop(1, nr)
    def _(k):
        r = lax.rem(r_me + k, nr)
        q_copy(r, r_me).wait_send()
        m_copy(r, r_me).wait_send()

    @pl.loop(0, nr)
    def _(k):
        r = lax.rem(r_me + k, nr)

        @pl.when(jnp.logical_or(r != r_me, home != p_me))
        def _():
            fr_copy(r, home, r_me, p_me).wait_send()

    for k in range(1, nc):
        fl_copy(lax.rem(p_me + k, nc), p_me).wait_send()

    @pl.loop(1, nd)
    def _(k):
        t = lax.rem(me + k, nd)
        b_copy(t // nc, lax.rem(t, nc), r_me, p_me).wait_send()
        for chunk in range(EDGE_CHUNKS):
            e_copy(chunk, t // nc, lax.rem(t, nc), r_me, p_me).wait_send()

    @pl.loop(1, nd)
    def _(k):
        t = lax.rem(me + k, nd)
        for chunk in range(EDGE_CHUNKS):
            e_copy(chunk, r_me, p_me, t // nc, lax.rem(t, nc)).wait_recv()

    def edge_blocks(row):
        blocks = []
        for b in range(nib):
            halves = [er[b, pl.ds(p * nr * rows_each + row, nr, stride=rows_each), :] for p in range(nc)]
            for n in range(per_lane):
                blocks.append(
                    jnp.concatenate([half[:, n * cb : (n + 1) * cb] for half in halves], axis=1)
                )
        return blocks

    some = crows // CROSS_CHUNKS

    def c_copy(chunk, r, p, origin):
        return copy(
            5 + EDGE_CHUNKS + chunk,
            cs.at[p, pl.ds(al(r * crows + chunk * some, some), some), :],
            cr.at[pl.ds(al(origin * crows + chunk * some, some), some), :],
            r * nc + p, origin, r, p,
        )

    def c_send(chunk):
        @pl.loop(1, nd)
        def _(k):
            t = lax.rem(me + k, nd)
            c_copy(chunk, t // nc, lax.rem(t, nc), me).start()

    for c in range(cpd):
        blocks = edge_blocks(c)
        left_rows = split(jnp.concatenate([blocks[i] for i in order], axis=0))
        right_rows = pick(perm_row_ref[...], split(jnp.concatenate(edge_blocks(cpd + c), axis=0)))
        crossed = dot_split(left_rows, right_rows, NT)
        for p in range(nc):
            half = crossed[:, p * cb : (p + 1) * cb]
            packed = jnp.concatenate(
                [half[n * nib * nr : (n + 1) * nib * nr] for n in range(per_lane)], axis=1
            )
            for b in range(nib):
                cs[p, pl.ds(c * nib + b, nr, stride=crows), :] = packed[b * nr : (b + 1) * nr]
        if (c + 1) % (cpd // CROSS_CHUNKS) == 0:
            c_send(c // (cpd // CROSS_CHUNKS))

    cr[pl.ds(al(me * crows, crows), crows), :] = cs[p_me, pl.ds(al(r_me * crows, crows), crows), :]

    @pl.loop(1, nd)
    def _(k):
        t = lax.rem(me + k, nd)
        for chunk in range(CROSS_CHUNKS):
            c_copy(chunk, t // nc, lax.rem(t, nc), me).wait_send()
            c_copy(chunk, r_me, p_me, t).wait_recv()

    tri_rows = []
    for b in range(nib):
        channels = cr[pl.ds(b, tri, stride=nib), :]
        tri_rows.append(dot_split(split(layer_norm(channels.T)), w_out))
    triangle = jnp.concatenate(tri_rows, axis=0) * out_gate
    pair_mid = pair_one + triangle
    hidden = jnp.maximum(dot_split(split(layer_norm(pair_mid)), w_in), 0.0)
    npair_ref[...] = (pair_mid + dot_split(split(hidden), w_back)).reshape(rb, cb, cz)


def fused(sizes, *args):
    (pair, ali, res_mask, row_mask, ain, pbw, aout, oin, oout, tin, tgate, tout, xin, xout) = args
    nb, np_, nc = sizes
    nr = nb * np_
    nd = nr * nc
    rb, cb, cz = pair.shape
    sb, _, cm = ali.shape
    res = rb * nr
    seq = sb * nc
    heads = pbw.shape[1]
    depth = aout.shape[0] // heads
    groups = nr // sb
    hpg = heads // groups
    gw = hpg * depth
    ow = oin.shape[1] // 2
    tri = tout.shape[0]
    cpd = tri // nd
    pos = rb * cb
    nib = pos // 128
    f32 = jnp.float32

    a = np.arange(seq * ow)
    perm_outer = np.zeros((seq * ow, seq * ow), np.float32)
    perm_outer[a, (a % ow) * seq + a // ow] = 1.0
    row = np.arange(2 * tri)
    channel = (row // cpd % 2) * 2 * tri + (row // (2 * cpd)) * cpd + row % cpd
    perm_gate = np.zeros((2 * tri, 4 * tri), np.float32)
    perm_gate[row, channel] = 1.0
    perm_value = np.zeros((2 * tri, 4 * tri), np.float32)
    perm_value[row, channel + tri] = 1.0
    n = np.arange(res)
    perm_row = np.zeros((res, res), np.float32)
    perm_row[n, (n % rb) * nr + n // rb] = 1.0
    position = np.arange(pos)
    pos_table = np.stack([position // cb, position % cb]).astype(np.int32)
    consts = [jnp.asarray(m, jnp.bfloat16) for m in (perm_outer, perm_gate, perm_value, perm_row)]
    operands = [
        pair, ali, res_mask.reshape(1, res), row_mask, ain, pbw.T, aout, oin.T, oout, tin, tgate, tout,
        xin, xout, *consts, jnp.asarray(pos_table),
    ]
    vmem = pl.BlockSpec(memory_space=pltpu.VMEM)
    fw = sb * ow + 128
    scratch = [
        ((nr, rb, 4 * gw)), ((res, 4 * gw)),
        ((heads * nib, 128)), ((nc, nr * hpg * nib, 128)),
        ((res, 128)), ((nr, rb, 128)),
        ((rb, fw)), ((nc, cb, fw)), ((rb, fw)), ((nc, rb, fw)),
        ((pos // 128, 2 * tri, 128)), ((pos // 128, 2 * tri, 128)),
        ((nc, nr * cpd * nib, 128)), ((tri * nib, 128)),
        ((rb * seq, 128)), ((rb, ow, seq, cz)), ((pos, cz)),
    ]
    return pl.pallas_call(
        functools.partial(block_kernel, sizes, len(operands)),
        out_shape=(
            jax.ShapeDtypeStruct(ali.shape, f32),
            jax.ShapeDtypeStruct(pair.shape, f32),
        ),
        in_specs=[pl.BlockSpec(memory_space=pltpu.HBM)] * len(operands),
        out_specs=(vmem, vmem),
        scratch_shapes=[pltpu.VMEM(m.shape, m.dtype) for m in operands]
        + [pltpu.VMEM(s, f32) for s in scratch]
        + [pltpu.VMEM((ow, 3 * ow, cz), jnp.bfloat16)]
        + [pltpu.SemaphoreType.DMA((5 + EDGE_CHUNKS + CROSS_CHUNKS, nd))] * 2
        + [pltpu.SemaphoreType.DMA((len(operands),))],
        compiler_params=pltpu.CompilerParams(
            collective_id=0, has_side_effects=True, vmem_limit_bytes=63 * 1024 * 1024
        ),
    )(*operands)


def fits(sizes, args):
    pair, ali, pbw, aout, oin, tout = (args[n] for n in (0, 1, 5, 6, 7, 11))
    nb, np_, nc = sizes
    nr = nb * np_
    rb, cb, cz = pair.shape
    sb = ali.shape[0]
    heads = pbw.shape[1]
    depth = aout.shape[0] // heads
    if nr % sb or heads % (nr // sb) or nr % nc or tout.shape[0] % (nr * nc):
        return False
    return (
        ali.shape[1] == rb and rb % 8 == 0 and cb * nc == rb * nr and 128 % cb == 0 and cz == 128
        and (sb * nc) % 8 == 0 and (2 * (tout.shape[0] // (nr * nc))) % 8 == 0
        and (heads // (nr // sb)) * depth * 4 % 128 == 0 and sb * (oin.shape[1] // 2) % 128 == 0
        and rb % (128 // cb) == 0 and (heads // (nr // sb)) * depth * 2 == 128
        and (heads // (nr // sb)) * (rb * cb // 128) % 8 == 0
        and tout.shape[0] // (nr * nc) * (rb * cb // 128) % (8 * CROSS_CHUNKS) == 0
        and (rb * cb // 128) % EDGE_CHUNKS == 0 and tout.shape[0] // (nr * nc) % CROSS_CHUNKS == 0
    )


def solution(mesh):
    sizes = tuple(mesh.shape[name] for name in ("branch", "prow", "pcol"))

    def local(*args):
        if fits(sizes, args):
            return fused(sizes, *args)
        return shards(*args)

    return jax.shard_map(
        local,
        mesh=mesh,
        in_specs=(
            P(("branch", "prow"), "pcol", None),
            P("pcol", ("branch", "prow"), None),
            P(),
            P("pcol", ("branch", "prow")),
            P(),
            P(),
            P(),
            P(),
            P(),
            P(),
            P(),
            P(),
            P(),
            P(),
        ),
        out_specs=(P("pcol", ("branch", "prow"), None), P(("branch", "prow"), "pcol", None)),
        check_vma=False,
    )
```
